128 devices in a mesh: dp: 16 (over y, x), expert: 4 (over z), et: 2 (over core).
Axes of the slice: x: 4, y: 4, z: 4, core: 2. Of those that a mesh axis runs over, the one named last changes fastest.
Arguments:
- tokens: bfloat16 [4096, 3072], P(('dp', 'expert'), 'et'), may hold values from -6 to 6
- expert_ids: int32 [4096, 2], P(('dp', 'expert')), may hold values from 0 to 3, all different within a row; in each aligned block of 64 rows (0 to 63, 64 to 127, ...) at most 40 rows name the same one
- gate_scores: float32 [4096, 2], P(('dp', 'expert')), may hold values from 0.1 to 1
- w_gate: bfloat16 [4, 3072, 8192], P('expert', None, ('dp', 'et')), may hold values from -0.109375 to 0.109375
- w_up: bfloat16 [4, 3072, 8192], P('expert', None, ('dp', 'et')), may hold values from -0.109375 to 0.109375
- w_down: bfloat16 [4, 8192, 3072], P('expert', 'dp', 'et'), may hold values from -0.0625 to 0.0625
Outputs:
- mixed: bfloat16 [4096, 3072], P(('dp', 'expert'), 'et')
The draws below stay inside these ranges and needn't reach their ends.
Inputs may be any that keep to these rules, and one draw needn't show every extreme that they name: `expert_ids`: the two experts of a token differ. Among the 64 tokens of one index pair of dp and expert (aligned blocks of rows) no expert is named more than 40 times, and in every draw some block names some expert exactly 40 times.
All inputs are finite; a program needn't handle non-finite values.
Results may differ from the reference program's by a relative error of at most 0.02.
Values may be sent and summed in bfloat16 or wider, within the bound.
No kernel may reach another device: no remote copies, remote signals or barrier semaphores. Data moves between devices by JAX's collectives and lax.ppermute only.
A program may use at most 128 MiB of HBM per device.

```python
import math
import jax
import jax.numpy as jnp
import numpy as np
from jax import lax

D = 3072
FF = 8192
TOK_DEV = 64
EXPERTS = 4
CAP = 40
TOKENS = 4096
N_DP = 16
N_EXPERT = 4


def steps_of(stream_key, extent, split, smallest, high):
    loudness, own = 1.0, jax.random.fold_in(stream_key, 6)
    for axis_at, shards_of in split:
        heights = jnp.exp(jax.random.uniform(jax.random.fold_in(own, axis_at), (shards_of,), jnp.float32, smallest / len(split), high / len(split)))
        loudness = loudness * jnp.repeat(heights, extent[axis_at] // shards_of).reshape([-1 if axis == axis_at else 1 for axis in range(len(extent))])
    return loudness


def assign_block(own_key, own, number, rows, amount, top, most, slope):
    ranking = jax.random.permutation(own_key, amount)
    crowded, common = load_shares(amount, rows * top, most, slope, True), load_shares(amount, rows * top, most, slope, False)
    places = jnp.arange(amount)

    def named(lengths, rotation):
        used = int((lengths > 0).sum())
        fixed = max(1, used // 4)
        passed = fixed + (places - fixed + rotation * (used - fixed)) % max(1, amount - fixed)
        return jnp.zeros((amount,), jnp.int32).at[ranking[jnp.where(places < fixed, places, passed)]].set(jnp.asarray(lengths, jnp.int32))

    lengths = jnp.where(number % 4 == 0, named(crowded, number // 4), named(common, number - number // 4 - 1))
    mixed = jax.random.permutation(jax.random.fold_in(own, 3), amount)
    giver, taker = mixed[0:amount // 2 * 2:2], mixed[1:amount // 2 * 2:2]
    margin = jnp.minimum(lengths[giver] - 1, most - lengths[taker]) // 2
    margin = jnp.where((giver == ranking[0]) | (taker == ranking[0]) | (lengths[taker] == 0), 0, jnp.maximum(margin, 0))
    passed = jax.random.randint(jax.random.fold_in(own, 4), (amount // 2,), 0, 1 << 20) % (margin + 1)
    lengths = lengths.at[giver].add(-passed).at[taker].add(passed)
    labels = jnp.searchsorted(jnp.cumsum(lengths), jnp.arange(rows * top), side="right").astype(jnp.int32)
    table = labels.reshape(top, rows).T
    table = table[jax.random.permutation(jax.random.fold_in(own, 1), rows)]
    rotation = jax.random.randint(jax.random.fold_in(own, 2), (rows, 1), 0, top)
    return jnp.take_along_axis(table, (jnp.arange(top)[None, :] + rotation) % top, axis=1)


def load_shares(number_of, total, most, skew, full):
    loads = [(1 << 20) // math.isqrt(standing ** skew) + 1 for standing in range(1, number_of + 1)]
    largest = most if full else min(most, max(-(-total // number_of), total * loads[0] // sum(loads)))
    least = 1 if total - largest >= number_of - 1 else 0
    counts, surplus = [largest] + [least] * (number_of - 1), total - largest - least * (number_of - 1)
    while surplus > 0:
        movable = [i for i in range(1, number_of) if counts[i] < largest] or [i for i in range(1, number_of) if counts[i] < most]
        whole, remaining = sum([loads[i] for i in movable]), surplus
        for i in movable:
            extra = min(most - counts[i], max(1, remaining * loads[i] // whole), surplus)
            counts[i] = counts[i] + extra
            surplus = surplus - extra
    return np.array(counts)


def normal_values(rng, extent, scale, most, cuts=(), kind=jnp.bfloat16):
    values = scale * jax.random.normal(rng, extent, jnp.float32)
    if cuts:
        values = values * steps_of(rng, extent, cuts, -0.22, 0.18)
    return jnp.clip(values, -most, most).astype(kind)


def setup_inputs(seed: int = 0) -> dict:
    key_of = jax.random.split(jax.random.key(seed), 7)
    tokens = normal_values(key_of[0], (TOKENS, D), 1.0, 6.0, ((0, 64), (1, 2)))
    expert_ids_keys = jax.random.split(jax.random.fold_in(key_of[1], 1), TOKENS // TOK_DEV)
    expert_ids_turns = jax.random.permutation(jax.random.fold_in(key_of[1], 3), TOKENS // TOK_DEV)
    expert_ids = jax.vmap(lambda own, number: assign_block(jax.random.fold_in(key_of[1], 2), own, number, TOK_DEV, EXPERTS, 2, CAP, 2))(expert_ids_keys, expert_ids_turns).reshape((TOKENS, 2))
    gate_scores = jnp.clip(0.1 + 0.9 * jax.random.uniform(key_of[2], (TOKENS, 2), jnp.float32) ** steps_of(key_of[2], (TOKENS, 2), ((0, 64),), -0.2, 0.2), 0.1, 1.0)
    w_gate = normal_values(key_of[3], (EXPERTS, D, FF), D ** -0.5, 0.109375, ((0, 4), (2, 32)))
    w_up = normal_values(key_of[4], (EXPERTS, D, FF), D ** -0.5, 0.109375, ((0, 4), (2, 32)))
    w_down = normal_values(key_of[5], (EXPERTS, FF, D), FF ** -0.5, 0.0625, ((0, 4), (1, 16), (2, 2)))
    return {"tokens": tokens, "expert_ids": expert_ids, "gate_scores": gate_scores, "w_gate": w_gate, "w_up": w_up, "w_down": w_down}


def reference(tokens, expert_ids, gate_scores, w_gate, w_up, w_down):
    flat = expert_ids.reshape(-1)
    onehot = (flat[:, None] == jnp.arange(EXPERTS, dtype=jnp.int32)[None, :]).astype(jnp.int32)
    before = jnp.cumsum(onehot, axis=0) - onehot
    rank = jnp.sum(before * onehot, axis=1).astype(jnp.int32)
    limit = CAP * N_DP * N_EXPERT
    block = FF // N_DP

    def expert_pass(index):
        chosen = jnp.nonzero(flat == index, size=limit, fill_value=0)[0].astype(jnp.int32)
        rows = tokens[chosen // 2]
        gate = jnp.dot(rows, w_gate[index], preferred_element_type=jnp.float32)
        up = jnp.dot(rows, w_up[index], preferred_element_type=jnp.float32)
        hidden = (jax.nn.silu(gate) * up).astype(jnp.bfloat16)
        hidden_blocks = jnp.transpose(hidden.reshape(limit, N_DP, block), (1, 0, 2))
        down_blocks = w_down[index].reshape(N_DP, block, D)

        def add_block(total, pair):
            part = jnp.dot(pair[0], pair[1], preferred_element_type=jnp.float32).astype(jnp.bfloat16)
            return total + part.astype(jnp.float32), None

        start = jnp.zeros((limit, D), jnp.float32)
        total, unused = lax.scan(add_block, start, (hidden_blocks, down_blocks))
        return total.astype(jnp.bfloat16)

    outputs = lax.map(expert_pass, jnp.arange(EXPERTS, dtype=jnp.int32))
    picked = outputs[flat, rank].astype(jnp.float32)
    weighted = picked * gate_scores.reshape(-1)[:, None]
    return weighted.reshape(-1, 2, D).sum(axis=1).astype(jnp.bfloat16)
```

```python
import jax
import jax.numpy as jnp
from jax import lax
from jax.experimental import pallas as pl
from jax.experimental.pallas import tpu as pltpu
from jax.sharding import PartitionSpec as P

SIDE = 4
BF = jnp.bfloat16
F32 = jnp.float32


def plane_perm(first, step):
    pairs = []
    for y in range(SIDE):
        for x in range(SIDE):
            for c in range(2):
                along_x = (c == 0) == first
                ty, tx = (y, (x + step) % SIDE) if along_x else ((y + step) % SIDE, x)
                pairs.append(((y * SIDE + x) * 2 + c, (ty * SIDE + tx) * 2 + c))
    return pairs


def shift(a, first, step):
    return lax.ppermute(a, ("dp", "et"), plane_perm(first, step))


def swap(a):
    return lax.ppermute(a, "et", [(0, 1), (1, 0)])


def gather_ring(a, first):
    half = a.shape[1] // 2
    left = shift(a, first, 1)
    right = shift(a, first, -1)
    far_a = shift(left[:, :half], first, 1)
    far_b = shift(right[:, half:], first, -1)
    return a, left, right, far_a, far_b


def add(*terms):
    total = terms[0].astype(F32)
    for t in terms[1:]:
        total = total + t.astype(F32)
    return total.astype(BF)


def scatter_ring(own, left, right, far_a, far_b, first):
    half = far_a.shape[1]
    got_a = shift(far_a, first, 1)
    got_b = shift(far_b, first, -1)
    right = jnp.concatenate([add(right[:, :half], got_a), right[:, half:]], axis=1)
    left = jnp.concatenate([left[:, :half], add(left[:, half:], got_b)], axis=1)
    from_left = shift(right, first, 1)
    from_right = shift(left, first, -1)
    return add(own, from_left, from_right)


def ffn_body(core, own, left, right, far_a, far_b, wg0, wg1, wu0, wu1, wd0, wd1,
             p_own, p_left, p_right, p_far_a, p_far_b, rows, hidden):
    c = core[0]
    n = own.shape[0]
    half = far_a.shape[1]
    hid = wg0.shape[1]
    rows[pl.ds(0, n), :] = own[...]
    rows[pl.ds(n, n), :] = left[...]
    rows[pl.ds(2 * n, n), :] = right[...]
    rows[pl.ds(3 * n, n), pl.ds(0, half)] = far_a[...]
    rows[pl.ds(3 * n, n), pl.ds(half, half)] = far_b[...]
    mine = pl.multiple_of(c * half, half)
    other = pl.multiple_of((1 - c) * half, half)

    def up_step(i, carry):
        at = pl.ds(pl.multiple_of(i * 2 * n, 2 * n), 2 * n)
        for k, (wg, wu) in enumerate(((wg0, wu0), (wg1, wu1))):
            def proj(w):
                return jnp.dot(
                    rows[at, pl.ds(0, half)], w[pl.ds(mine, half), :], preferred_element_type=F32
                ) + jnp.dot(
                    rows[at, pl.ds(half, half)], w[pl.ds(other, half), :], preferred_element_type=F32
                )

            g = proj(wg)
            u = proj(wu)
            hidden[at, pl.ds(k * hid, hid)] = (g / (1.0 + jnp.exp(-g)) * u).astype(BF)
        return carry

    lax.fori_loop(0, 2, up_step, 0)
    mine_h = pl.multiple_of(c * hid, hid)
    other_h = pl.multiple_of((1 - c) * hid, hid)

    def down(first, w):
        h = hidden[pl.ds(first, 2 * n), :]
        return jnp.dot(h[:, :hid], w[pl.ds(mine_h, hid), :], preferred_element_type=F32) + jnp.dot(
            h[:, hid:], w[pl.ds(other_h, hid), :], preferred_element_type=F32
        )

    a = down(0, wd0)
    p_own[:, pl.ds(0, half)] = a[:n].astype(BF)
    p_left[:, pl.ds(0, half)] = a[n:].astype(BF)
    a = down(0, wd1)
    p_own[:, pl.ds(half, half)] = a[:n].astype(BF)
    p_left[:, pl.ds(half, half)] = a[n:].astype(BF)
    a = down(2 * n, wd0)
    p_right[:, pl.ds(0, half)] = a[:n].astype(BF)
    p_far_a[...] = a[n:].astype(BF)
    a = down(2 * n, wd1)
    p_right[:, pl.ds(half, half)] = a[:n].astype(BF)
    p_far_b[...] = a[n:].astype(BF)


def ffn(core, groups, weights):
    n, d = groups[0].shape
    half = d // 2
    hid = weights[0].shape[1]
    whole = pl.BlockSpec(memory_space=pltpu.VMEM)
    full = jax.ShapeDtypeStruct((n, d), BF)
    part = jax.ShapeDtypeStruct((n, half), BF)
    return pl.pallas_call(
        ffn_body,
        in_specs=[pl.BlockSpec(memory_space=pltpu.SMEM)] + [whole] * 11,
        out_specs=[whole] * 5,
        out_shape=[full, full, full, part, part],
        scratch_shapes=[pltpu.VMEM((4 * n, d), BF), pltpu.VMEM((4 * n, 2 * hid), BF)],
        compiler_params=pltpu.CompilerParams(vmem_limit_bytes=48 * 1024 * 1024),
        cost_estimate=pl.CostEstimate(
            flops=2 * 4 * n * d * hid * 6, bytes_accessed=16 * n * d + 12 * d * hid,
            transcendentals=8 * n * hid,
        ),
        name="ffn",
    )(core, *groups, *weights)


def on_device(tokens, expert_ids, gate_scores, w_gate, w_up, w_down):
    tok_rows, half = tokens.shape
    n_expert = lax.axis_size("expert")
    capacity = max(2, 5 * tok_rows // (2 * n_expert))
    z = lax.axis_index("expert")
    c = lax.axis_index("et")
    core = c.astype(jnp.int32).reshape(1)

    other_tokens = swap(tokens)
    weights = []
    for w in (w_gate[0], w_up[0], w_down[0]):
        weights += [w, swap(w)]

    t = jnp.arange(tok_rows, dtype=jnp.int32)
    slots = jnp.arange(capacity, dtype=jnp.int32)
    before = (t[:, None] < t[None, :]).astype(F32)

    def choose(e):
        named = expert_ids == e
        mask = jnp.any(named, axis=1)
        rank = jnp.dot(mask.astype(F32)[None, :], before, preferred_element_type=F32)[0].astype(jnp.int32)
        pick = (slots[:, None] == rank[None, :]) & mask[None, :]
        return pick.astype(BF), jnp.sum(jnp.where(named, gate_scores, 0.0), axis=1)

    send = [
        [(s * 2, s * 2) for s in range(n_expert)] + [(s * 2 + 1, (s - 1) % n_expert * 2 + 1) for s in range(n_expert)],
        [(s * 2, (s + 2) % n_expert * 2) for s in range(n_expert)]
        + [(s * 2 + 1, (s + 1) % n_expert * 2 + 1) for s in range(n_expert)],
    ]
    picks = [choose((z - c) % n_expert), choose((z + 2 - c) % n_expert)]

    arrived = []
    for (pick, _), pairs in zip(picks, send):
        out = jnp.concatenate(
            [jnp.dot(pick, v, preferred_element_type=F32).astype(BF) for v in (tokens, other_tokens)], axis=1
        )
        arrived.append(lax.ppermute(out, ("expert", "et"), pairs))

    total = jnp.zeros((tok_rows, 2 * half), F32)
    for a, (pick, score), pairs in zip(arrived, picks, send):
        own, left, right, far_a, far_b = gather_ring(a, True)
        line = jnp.concatenate([own, left, right, jnp.concatenate([far_a, far_b], axis=1)], axis=0)
        parts = ffn(core, gather_ring(line, False), weights)
        s = scatter_ring(*parts, False).reshape(SIDE, capacity, 2 * half)
        done = scatter_ring(s[0], s[1], s[2], s[3, :, :half], s[3, :, half:], True)
        back = lax.ppermute(done, ("expert", "et"), [(b, a_) for a_, b in pairs])
        rows = lax.dot_general(pick, back, (((0,), (0,)), ((), ())), preferred_element_type=F32)
        total = total + rows * score[:, None]
    theirs = swap(total[:, half:].astype(BF))
    return (total[:, :half] + theirs.astype(F32)).astype(BF)


def solution(mesh):
    placed = (
        P(("dp", "expert"), "et"),
        P(("dp", "expert"), None),
        P(("dp", "expert"), None),
        P("expert", None, ("dp", "et")),
        P("expert", None, ("dp", "et")),
        P("expert", "dp", "et"),
    )
    return jax.shard_map(
        on_device, mesh=mesh, in_specs=placed, out_specs=P(("dp", "expert"), "et"), check_vma=False
    )
```

```python
import jax
import jax.numpy as jnp
from jax import lax
from jax.experimental import pallas as pl
from jax.experimental.pallas import tpu as pltpu
from jax.sharding import PartitionSpec as P

SIDE = 4
BF = jnp.bfloat16
F32 = jnp.float32
VMEM_MB = 16


def plane_perm(first, step):
    pairs = []
    for y in range(SIDE):
        for x in range(SIDE):
            for c in range(2):
                along_x = (c == 0) == first
                ty, tx = (y, (x + step) % SIDE) if along_x else ((y + step) % SIDE, x)
                pairs.append(((y * SIDE + x) * 2 + c, (ty * SIDE + tx) * 2 + c))
    return pairs


def shift(a, first, step):
    return lax.ppermute(a, ("dp", "et"), plane_perm(first, step))


def swap(a):
    return lax.ppermute(a, "et", [(0, 1), (1, 0)])


def tie(value, *after):
    return lax.optimization_barrier((value, *after))[0]


def both(plus, minus, first):
    return shift(plus, first, 1), shift(minus, first, -1)


def add(*terms):
    total = terms[0].astype(F32)
    for t in terms[1:]:
        total = total + t.astype(F32)
    return total.astype(BF)


def ffn_body(core, *refs):
    c = core[0]
    wg0, wg1, wu0, wu1, wd0, wd1 = refs[:6]
    hidden = refs[-1]
    n_arrays = (len(refs) - 7) // 2
    ins, outs = refs[6:6 + n_arrays], refs[6 + n_arrays:-1]
    d = 2 * wd0.shape[1]
    half = d // 2
    hid = wg0.shape[1]
    mine = pl.multiple_of(c * half, half)
    other = pl.multiple_of((1 - c) * half, half)
    mine_h = pl.multiple_of(c * hid, hid)
    other_h = pl.multiple_of((1 - c) * hid, hid)
    lo, hi = pl.ds(0, half), pl.ds(half, half)
    at = 0
    while at < n_arrays:
        if ins[at].shape[1] == d:
            a, b = ins[at][:, lo], ins[at][:, hi]
            halves = [(outs[at], lo), (outs[at], hi)]
            at += 1
        else:
            a, b = ins[at][...], ins[at + 1][...]
            halves = [(outs[at], lo), (outs[at + 1], lo)]
            at += 2
        for k, (wg, wu) in enumerate(((wg0, wu0), (wg1, wu1))):
            def proj(w):
                return jnp.dot(a, w[pl.ds(mine, half), :], preferred_element_type=F32) + jnp.dot(
                    b, w[pl.ds(other, half), :], preferred_element_type=F32
                )

            g = proj(wg)
            u = proj(wu)
            hidden[:, pl.ds(k * hid, hid)] = (g / (1.0 + jnp.exp(-g)) * u).astype(BF)
        h0, h1 = hidden[:, pl.ds(0, hid)], hidden[:, pl.ds(hid, hid)]
        for (out, cols), w, first, second in zip(halves, (wd0, wd1), (mine_h, 0), (other_h, hid)):
            p = jnp.dot(h0, w[pl.ds(first, hid), :], preferred_element_type=F32) + jnp.dot(
                h1, w[pl.ds(second, hid), :], preferred_element_type=F32
            )
            out[:, cols] = p.astype(BF)


def ffn(core, weights, arrays):
    n = arrays[0].shape[0]
    half = weights[4].shape[1]
    hid = weights[0].shape[1]
    rows = sum(a.size for a in arrays) // (2 * half)
    whole = pl.BlockSpec(memory_space=pltpu.VMEM)
    return pl.pallas_call(
        ffn_body,
        in_specs=[pl.BlockSpec(memory_space=pltpu.SMEM)] + [whole] * (6 + len(arrays)),
        out_specs=[whole] * len(arrays),
        out_shape=[jax.ShapeDtypeStruct(a.shape, BF) for a in arrays],
        scratch_shapes=[pltpu.VMEM((n, 2 * hid), BF)],
        compiler_params=pltpu.CompilerParams(vmem_limit_bytes=VMEM_MB * 1024 * 1024),
        cost_estimate=pl.CostEstimate(
            flops=2 * rows * half * 2 * hid * 6, bytes_accessed=8 * rows * half + 24 * half * hid,
            transcendentals=2 * rows * hid,
        ),
        name="ffn",
    )(core, *weights, *arrays)


def on_device(tokens, expert_ids, gate_scores, w_gate, w_up, w_down):
    tok_rows, half = tokens.shape
    n_expert = lax.axis_size("expert")
    capacity = max(2, 5 * tok_rows // (2 * n_expert))
    z = lax.axis_index("expert")
    c = lax.axis_index("et")
    core = c.astype(jnp.int32).reshape(1)

    other_tokens = swap(tokens)
    t = jnp.arange(tok_rows, dtype=jnp.int32)
    slots = jnp.arange(capacity, dtype=jnp.int32)
    before = (t[:, None] < t[None, :]).astype(F32)

    def choose(e):
        named = expert_ids == e
        mask = jnp.any(named, axis=1)
        rank = jnp.dot(mask.astype(F32)[None, :], before, preferred_element_type=F32)[0].astype(jnp.int32)
        pick = (slots[:, None] == rank[None, :]) & mask[None, :]
        return pick.astype(BF), jnp.sum(jnp.where(named, gate_scores, 0.0), axis=1)

    send = [
        [(s * 2, s * 2) for s in range(n_expert)] + [(s * 2 + 1, (s - 1) % n_expert * 2 + 1) for s in range(n_expert)],
        [(s * 2, (s + 2) % n_expert * 2) for s in range(n_expert)]
        + [(s * 2 + 1, (s + 1) % n_expert * 2 + 1) for s in range(n_expert)],
    ]
    picks = [choose((z - c) % n_expert), choose((z + 2 - c) % n_expert)]

    pick_all = jnp.concatenate([pick for pick, _ in picks], axis=0)
    outgoing = jnp.concatenate(
        [jnp.dot(pick_all, v, preferred_element_type=F32).astype(BF) for v in (tokens, other_tokens)], axis=1
    )

    def dispatch(k):
        return lax.ppermute(outgoing[k * capacity:(k + 1) * capacity], ("expert", "et"), send[k])

    def far_pair(left, right, first):
        return both(left[:, :half], right[:, half:], first)

    def fold(left, right, got_a, got_b):
        return (
            jnp.concatenate([left[:, :half], add(left[:, half:], got_b)], axis=1),
            jnp.concatenate([add(right[:, :half], got_a), right[:, half:]], axis=1),
        )

    weights = []
    for w in (w_down[0], w_up[0], w_gate[0]):
        weights = [w, swap(w)] + weights
    hid = w_gate.shape[2]
    down = weights[5]
    weights[5] = jnp.where(c == 0, down, jnp.concatenate([down[hid:], down[:hid]], axis=0))
    z0 = dispatch(0)
    z1 = dispatch(1)

    def spread(own):
        left, right, far = shift(own, True, 1), shift(own, True, -1), shift(own, True, 2)
        return jnp.concatenate([own, left, right, far], axis=0)

    def collect(sums):
        own, left, right, far = sums.reshape(SIDE, capacity, 2 * half)
        return add(own, shift(left, True, -1), shift(right, True, 1), shift(far, True, 2))

    line0 = spread(tie(z0, z1, *weights))
    line1 = spread(tie(z1, line0))
    left0, right0 = both(line0, line0, False)
    (p_own0,) = ffn(core, weights, (line0,))
    line1 = tie(line1, p_own0)
    left1, right1 = both(line1, line1, False)
    far_a0, far_b0 = far_pair(left0, right0, False)
    p_left0, p_right0 = ffn(core, weights, (left0, right0))
    (p_own1,) = ffn(core, weights, (tie(line1, p_left0),))
    far_a1, far_b1 = far_pair(tie(left1, p_own1), right1, False)
    p_left1, p_right1 = ffn(core, weights, (left1, right1))
    pf_a0, pf_b0 = ffn(core, weights, (tie(far_a0, p_left1), far_b0))
    got_a0, got_b0 = both(pf_a0, pf_b0, False)
    pf_a1, pf_b1 = ffn(core, weights, (tie(far_a1, pf_a0), far_b1))
    got_a1, got_b1 = both(pf_a1, pf_b1, False)
    sl0, sr0 = fold(p_left0, p_right0, got_a0, got_b0)
    from_l0, from_r0 = both(sr0, sl0, False)
    sl1, sr1 = fold(p_left1, p_right1, got_a1, got_b1)
    from_l1, from_r1 = both(sr1, sl1, False)
    done0 = collect(add(p_own0, from_l0, from_r0))
    done1 = collect(add(p_own1, from_l1, from_r1))
    back0 = lax.ppermute(done0, ("expert", "et"), [(b, a) for a, b in send[0]])
    back1 = lax.ppermute(tie(done1, back0), ("expert", "et"), [(b, a) for a, b in send[1]])

    total = jnp.zeros((tok_rows, 2 * half), F32)
    for back, (pick, score) in zip((back0, back1), picks):
        rows = lax.dot_general(pick, back, (((0,), (0,)), ((), ())), preferred_element_type=F32)
        total = total + rows * score[:, None]
    theirs = swap(total[:, half:].astype(BF))
    return (total[:, :half] + theirs.astype(F32)).astype(BF)


def solution(mesh):
    placed = (
        P(("dp", "expert"), "et"),
        P(("dp", "expert"), None),
        P(("dp", "expert"), None),
        P("expert", None, ("dp", "et")),
        P("expert", None, ("dp", "et")),
        P("expert", "dp", "et"),
    )
    return jax.shard_map(
        on_device, mesh=mesh, in_specs=placed, out_specs=P(("dp", "expert"), "et"), check_vma=False
    )
```

```python
import jax
import jax.numpy as jnp
from jax import lax
from jax.experimental import pallas as pl
from jax.experimental.pallas import tpu as pltpu
from jax.sharding import PartitionSpec as P

SIDE = 4
BF = jnp.bfloat16
F32 = jnp.float32
VMEM_MB = 16


def plane_perm(first, step):
    pairs = []
    for y in range(SIDE):
        for x in range(SIDE):
            for c in range(2):
                along_x = (c == 0) == first
                ty, tx = (y, (x + step) % SIDE) if along_x else ((y + step) % SIDE, x)
                pairs.append(((y * SIDE + x) * 2 + c, (ty * SIDE + tx) * 2 + c))
    return pairs


def shift(a, first, step):
    return lax.ppermute(a, ("dp", "et"), plane_perm(first, step))


def swap(a):
    return lax.ppermute(a, "et", [(0, 1), (1, 0)])


def tie(value, *after):
    return lax.optimization_barrier((value, *after))[0]


def both(plus, minus, first):
    return shift(plus, first, 1), shift(minus, first, -1)


def add(*terms):
    total = terms[0].astype(F32)
    for t in terms[1:]:
        total = total + t.astype(F32)
    return total.astype(BF)


def ffn_body(core, *refs):
    c = core[0]
    wg0, wg1, wu0, wu1, wd0, wd1 = refs[:6]
    hidden = refs[-1]
    n_arrays = (len(refs) - 7) // 2
    ins, outs = refs[6:6 + n_arrays], refs[6 + n_arrays:-1]
    d = 2 * wd0.shape[1]
    half = d // 2
    hid = wg0.shape[1]
    mine = pl.multiple_of(c * half, half)
    other = pl.multiple_of((1 - c) * half, half)
    mine_h = pl.multiple_of(c * hid, hid)
    other_h = pl.multiple_of((1 - c) * hid, hid)
    lo, hi = pl.ds(0, half), pl.ds(half, half)
    at = 0
    while at < n_arrays:
        if ins[at].shape[1] == d:
            a, b = ins[at][:, lo], ins[at][:, hi]
            halves = [(outs[at], lo), (outs[at], hi)]
            at += 1
        else:
            a, b = ins[at][...], ins[at + 1][...]
            halves = [(outs[at], lo), (outs[at + 1], lo)]
            at += 2
        for k, (wg, wu) in enumerate(((wg0, wu0), (wg1, wu1))):
            def proj(w):
                return jnp.dot(a, w[pl.ds(mine, half), :], preferred_element_type=F32) + jnp.dot(
                    b, w[pl.ds(other, half), :], preferred_element_type=F32
                )

            g = proj(wg)
            u = proj(wu)
            hidden[:, pl.ds(k * hid, hid)] = (g / (1.0 + jnp.exp(-g)) * u).astype(BF)
        h0, h1 = hidden[:, pl.ds(0, hid)], hidden[:, pl.ds(hid, hid)]
        for (out, cols), w, first, second in zip(halves, (wd0, wd1), (mine_h, 0), (other_h, hid)):
            p = jnp.dot(h0, w[pl.ds(first, hid), :], preferred_element_type=F32) + jnp.dot(
                h1, w[pl.ds(second, hid), :], preferred_element_type=F32
            )
            out[:, cols] = p.astype(BF)


def ffn(core, weights, arrays):
    n = arrays[0].shape[0]
    half = weights[4].shape[1]
    hid = weights[0].shape[1]
    rows = sum(a.size for a in arrays) // (2 * half)
    whole = pl.BlockSpec(memory_space=pltpu.VMEM)
    return pl.pallas_call(
        ffn_body,
        in_specs=[pl.BlockSpec(memory_space=pltpu.SMEM)] + [whole] * (6 + len(arrays)),
        out_specs=[whole] * len(arrays),
        out_shape=[jax.ShapeDtypeStruct(a.shape, BF) for a in arrays],
        scratch_shapes=[pltpu.VMEM((n, 2 * hid), BF)],
        compiler_params=pltpu.CompilerParams(vmem_limit_bytes=VMEM_MB * 1024 * 1024),
        cost_estimate=pl.CostEstimate(
            flops=2 * rows * half * 2 * hid * 6, bytes_accessed=8 * rows * half + 24 * half * hid,
            transcendentals=2 * rows * hid,
        ),
        name="ffn",
    )(core, *weights, *arrays)


def on_device(tokens, expert_ids, gate_scores, w_gate, w_up, w_down):
    tok_rows, half = tokens.shape
    n_expert = lax.axis_size("expert")
    capacity = max(2, 5 * tok_rows // (2 * n_expert))
    z = lax.axis_index("expert")
    c = lax.axis_index("et")
    core = c.astype(jnp.int32).reshape(1)

    other_tokens = swap(tokens)
    t = jnp.arange(tok_rows, dtype=jnp.int32)
    slots = jnp.arange(capacity, dtype=jnp.int32)
    before = (t[:, None] < t[None, :]).astype(F32)

    def choose(e):
        named = expert_ids == e
        mask = jnp.any(named, axis=1)
        rank = jnp.dot(mask.astype(F32)[None, :], before, preferred_element_type=F32)[0].astype(jnp.int32)
        pick = (slots[:, None] == rank[None, :]) & mask[None, :]
        return pick.astype(BF), jnp.sum(jnp.where(named, gate_scores, 0.0), axis=1)

    send = [
        [(s * 2, s * 2) for s in range(n_expert)] + [(s * 2 + 1, (s - 1) % n_expert * 2 + 1) for s in range(n_expert)],
        [(s * 2, (s + 2) % n_expert * 2) for s in range(n_expert)]
        + [(s * 2 + 1, (s + 1) % n_expert * 2 + 1) for s in range(n_expert)],
    ]
    picks = [choose((z - c) % n_expert), choose((z + 2 - c) % n_expert)]

    pick_all = jnp.concatenate([pick for pick, _ in picks], axis=0)
    outgoing = jnp.concatenate(
        [jnp.dot(pick_all, v, preferred_element_type=F32).astype(BF) for v in (tokens, other_tokens)], axis=1
    )

    def dispatch(k, *after):
        rows = outgoing[k * capacity:(k + 1) * capacity]
        return lax.ppermute(tie(rows, *after) if after else rows, ("expert", "et"), send[k])

    def far_pair(left, right, first):
        return both(left[:, :half], right[:, half:], first)

    def fold(left, right, got_a, got_b):
        return (
            jnp.concatenate([left[:, :half], add(left[:, half:], got_b)], axis=1),
            jnp.concatenate([add(right[:, :half], got_a), right[:, half:]], axis=1),
        )

    z0 = dispatch(0)
    z1 = dispatch(1)
    weights = []
    for w in (w_gate[0], w_up[0], w_down[0]):
        weights += [w, swap(tie(w, other_tokens))]

    def collect(sums, *after):
        own, left, right, far = sums.reshape(SIDE, capacity, 2 * half)
        own = tie(own, *after) if after else own
        return add(own, shift(left, True, -1), shift(right, True, 1), shift(far, True, 2))

    own = tie(jnp.concatenate([z0, z1], axis=0), *weights)
    ring = (own, shift(own, True, 1), shift(own, True, -1), shift(own, True, 2))
    line0, line1 = [
        jnp.concatenate([p[k * capacity:(k + 1) * capacity] for p in ring], axis=0) for k in range(2)
    ]
    hid = w_gate.shape[2]
    down = tie(weights[5], own)
    weights[5] = jnp.where(c == 0, down, jnp.concatenate([down[hid:], down[:hid]], axis=0))
    left0, right0 = both(line0, line0, False)
    left1, right1 = both(line1, line1, False)
    (p_own0,) = ffn(core, weights, (line0,))
    (p_own1,) = ffn(core, weights, (line1,))
    left0, right0 = tie(left0, p_own0, p_own1), tie(right0, p_own0, p_own1)
    far_a0, far_b0 = far_pair(left0, right0, False)
    p_left0, p_right0 = ffn(core, weights, (left0, right0))
    far_a1, far_b1 = far_pair(tie(left1, p_left0), tie(right1, p_left0), False)
    p_left1, p_right1 = ffn(core, weights, (left1, right1))
    pf_a0, pf_b0 = ffn(core, weights, (tie(far_a0, p_left1), far_b0))
    got_a0, got_b0 = both(pf_a0, pf_b0, False)
    pf_a1, pf_b1 = ffn(core, weights, (tie(far_a1, pf_a0), far_b1))
    got_a1, got_b1 = both(pf_a1, pf_b1, False)
    sl0, sr0 = fold(p_left0, p_right0, got_a0, got_b0)
    from_l0, from_r0 = both(sr0, sl0, False)
    sl1, sr1 = fold(p_left1, p_right1, got_a1, got_b1)
    from_l1, from_r1 = both(sr1, sl1, False)
    done0 = collect(add(p_own0, from_l0, from_r0))
    back0 = lax.ppermute(done0, ("expert", "et"), [(b, a) for a, b in send[0]])
    done1 = collect(tie(add(p_own1, from_l1, from_r1), done0), back0)
    back1 = lax.ppermute(done1, ("expert", "et"), [(b, a) for a, b in send[1]])

    def combine(cols):
        total = jnp.zeros((tok_rows, half), F32)
        for back, (pick, score) in zip((back0, back1), picks):
            rows = lax.dot_general(pick, back[:, cols], (((0,), (0,)), ((), ())), preferred_element_type=F32)
            total = total + rows * score[:, None]
        return total

    theirs = swap(combine(slice(half, 2 * half)).astype(BF))
    return (combine(slice(0, half)) + theirs.astype(F32)).astype(BF)


def solution(mesh):
    placed = (
        P(("dp", "expert"), "et"),
        P(("dp", "expert"), None),
        P(("dp", "expert"), None),
        P("expert", None, ("dp", "et")),
        P("expert", None, ("dp", "et")),
        P("expert", "dp", "et"),
    )
    return jax.shard_map(
        on_device, mesh=mesh, in_specs=placed, out_specs=P(("dp", "expert"), "et"), check_vma=False
    )
```

```python
import jax
import jax.numpy as jnp
from jax import lax
from jax.experimental import pallas as pl
from jax.experimental.pallas import tpu as pltpu
from jax.sharding import PartitionSpec as P

SIDE = 4
BF = jnp.bfloat16
F32 = jnp.float32
VMEM_MB = 16


def plane_perm(first, step):
    pairs = []
    for y in range(SIDE):
        for x in range(SIDE):
            for c in range(2):
                along_x = (c == 0) == first
                ty, tx = (y, (x + step) % SIDE) if along_x else ((y + step) % SIDE, x)
                pairs.append(((y * SIDE + x) * 2 + c, (ty * SIDE + tx) * 2 + c))
    return pairs


def shift(a, first, step):
    return lax.ppermute(a, ("dp", "et"), plane_perm(first, step))


def swap(a):
    return lax.ppermute(a, "et", [(0, 1), (1, 0)])


def tie(value, *after):
    return lax.optimization_barrier((value, *after))[0]


def both(plus, minus, first):
    return shift(plus, first, 1), shift(minus, first, -1)


def add(*terms):
    total = terms[0].astype(F32)
    for t in terms[1:]:
        total = total + t.astype(F32)
    return total.astype(BF)


def ffn_body(core, *refs):
    c = core[0]
    wg0, wg1, wu0, wu1, wd0, wd1 = refs[:6]
    hidden = refs[-1]
    n_arrays = (len(refs) - 7) // 2
    ins, outs = refs[6:6 + n_arrays], refs[6 + n_arrays:-1]
    d = 2 * wd0.shape[1]
    half = d // 2
    hid = wg0.shape[1]
    mine = pl.multiple_of(c * half, half)
    other = pl.multiple_of((1 - c) * half, half)
    mine_h = pl.multiple_of(c * hid, hid)
    other_h = pl.multiple_of((1 - c) * hid, hid)
    lo, hi = pl.ds(0, half), pl.ds(half, half)
    at = 0
    while at < n_arrays:
        if ins[at].shape[1] == d:
            a, b = ins[at][:, lo], ins[at][:, hi]
            halves = [(outs[at], lo), (outs[at], hi)]
            at += 1
        else:
            a, b = ins[at][...], ins[at + 1][...]
            halves = [(outs[at], lo), (outs[at + 1], lo)]
            at += 2
        for k, (wg, wu) in enumerate(((wg0, wu0), (wg1, wu1))):
            def proj(w):
                return jnp.dot(a, w[pl.ds(mine, half), :], preferred_element_type=F32) + jnp.dot(
                    b, w[pl.ds(other, half), :], preferred_element_type=F32
                )

            g = proj(wg)
            u = proj(wu)
            hidden[:, pl.ds(k * hid, hid)] = (g / (1.0 + jnp.exp(-g)) * u).astype(BF)
        h0, h1 = hidden[:, pl.ds(0, hid)], hidden[:, pl.ds(hid, hid)]
        for (out, cols), w, first, second in zip(halves, (wd0, wd1), (mine_h, 0), (other_h, hid)):
            p = jnp.dot(h0, w[pl.ds(first, hid), :], preferred_element_type=F32) + jnp.dot(
                h1, w[pl.ds(second, hid), :], preferred_element_type=F32
            )
            out[:, cols] = p.astype(BF)


def ffn(core, weights, arrays):
    n = arrays[0].shape[0]
    half = weights[4].shape[1]
    hid = weights[0].shape[1]
    rows = sum(a.size for a in arrays) // (2 * half)
    whole = pl.BlockSpec(memory_space=pltpu.VMEM)
    return pl.pallas_call(
        ffn_body,
        in_specs=[pl.BlockSpec(memory_space=pltpu.SMEM)] + [whole] * (6 + len(arrays)),
        out_specs=[whole] * len(arrays),
        out_shape=[jax.ShapeDtypeStruct(a.shape, BF) for a in arrays],
        scratch_shapes=[pltpu.VMEM((n, 2 * hid), BF)],
        compiler_params=pltpu.CompilerParams(vmem_limit_bytes=VMEM_MB * 1024 * 1024),
        cost_estimate=pl.CostEstimate(
            flops=2 * rows * half * 2 * hid * 6, bytes_accessed=8 * rows * half + 24 * half * hid,
            transcendentals=2 * rows * hid,
        ),
        name="ffn",
    )(core, *weights, *arrays)


def on_device(tokens, expert_ids, gate_scores, w_gate, w_up, w_down):
    tok_rows, half = tokens.shape
    n_expert = lax.axis_size("expert")
    capacity = max(2, 5 * tok_rows // (2 * n_expert))
    z = lax.axis_index("expert")
    c = lax.axis_index("et")
    core = c.astype(jnp.int32).reshape(1)

    other_tokens = swap(tokens)
    t = jnp.arange(tok_rows, dtype=jnp.int32)
    slots = jnp.arange(capacity, dtype=jnp.int32)
    before = (t[:, None] < t[None, :]).astype(F32)

    def choose(e):
        named = expert_ids == e
        mask = jnp.any(named, axis=1)
        rank = jnp.dot(mask.astype(F32)[None, :], before, preferred_element_type=F32)[0].astype(jnp.int32)
        pick = (slots[:, None] == rank[None, :]) & mask[None, :]
        return pick.astype(BF), jnp.sum(jnp.where(named, gate_scores, 0.0), axis=1)

    send = [
        [(s * 2, (s + 2) % n_expert * 2) for s in range(n_expert)]
        + [(s * 2 + 1, (s + 1) % n_expert * 2 + 1) for s in range(n_expert)],
        [(s * 2, s * 2) for s in range(n_expert)] + [(s * 2 + 1, (s - 1) % n_expert * 2 + 1) for s in range(n_expert)],
    ]
    picks = [choose((z + 2 - c) % n_expert), choose((z - c) % n_expert)]

    pick_all = jnp.concatenate([pick for pick, _ in picks], axis=0)
    outgoing = jnp.concatenate(
        [jnp.dot(pick_all, v, preferred_element_type=F32).astype(BF) for v in (tokens, other_tokens)], axis=1
    )

    def dispatch(k, *after):
        rows = outgoing[k * capacity:(k + 1) * capacity]
        return lax.ppermute(tie(rows, *after) if after else rows, ("expert", "et"), send[k])

    def far_pair(left, right, first):
        return both(left[:, :half], right[:, half:], first)

    def fold(left, right, got_a, got_b):
        return (
            jnp.concatenate([left[:, :half], add(left[:, half:], got_b)], axis=1),
            jnp.concatenate([add(right[:, :half], got_a), right[:, half:]], axis=1),
        )

    z1 = dispatch(1)
    z0 = dispatch(0)
    weights = []
    for w in (w_gate[0], w_up[0], w_down[0]):
        weights += [w, swap(tie(w, other_tokens))]

    def collect(sums, *after):
        own, left, right, far = sums.reshape(SIDE, capacity, 2 * half)
        own = tie(own, *after) if after else own
        return add(own, shift(left, True, -1), shift(right, True, 1), shift(far, True, 2))

    own = tie(jnp.concatenate([z1, z0], axis=0), *weights)
    ring = (own, shift(own, True, 1), shift(own, True, -1), shift(own, True, 2))
    line0, line1 = [
        jnp.concatenate([p[k * capacity:(k + 1) * capacity] for p in ring], axis=0) for k in (1, 0)
    ]
    hid = w_gate.shape[2]
    down = tie(weights[5], own)
    weights[5] = jnp.where(c == 0, down, jnp.concatenate([down[hid:], down[:hid]], axis=0))
    left0, right0 = both(line0, line0, False)
    left1, right1 = both(line1, line1, False)
    (p_own0,) = ffn(core, weights, (line0,))
    (p_own1,) = ffn(core, weights, (line1,))
    left0, right0 = tie(left0, p_own0, p_own1), tie(right0, p_own0, p_own1)
    far_a0, far_b0 = far_pair(left0, right0, False)
    p_left0, p_right0 = ffn(core, weights, (left0, right0))
    far_a1, far_b1 = far_pair(tie(left1, p_left0), tie(right1, p_left0), False)
    p_left1, p_right1 = ffn(core, weights, (left1, right1))
    pf_a0, pf_b0 = ffn(core, weights, (tie(far_a0, p_left1), far_b0))
    got_a0, got_b0 = both(pf_a0, pf_b0, False)
    pf_a1, pf_b1 = ffn(core, weights, (tie(far_a1, pf_a0), far_b1))
    got_a1, got_b1 = both(pf_a1, pf_b1, False)
    sl0, sr0 = fold(p_left0, p_right0, got_a0, got_b0)
    from_l0, from_r0 = both(sr0, sl0, False)
    sl1, sr1 = fold(p_left1, p_right1, got_a1, got_b1)
    from_l1, from_r1 = both(sr1, sl1, False)
    done0 = collect(add(p_own0, from_l0, from_r0))
    back0 = lax.ppermute(done0, ("expert", "et"), [(b, a) for a, b in send[0]])
    done1 = collect(tie(add(p_own1, from_l1, from_r1), done0), back0)
    back1 = lax.ppermute(done1, ("expert", "et"), [(b, a) for a, b in send[1]])

    def combine(cols):
        total = jnp.zeros((tok_rows, half), F32)
        for back, (pick, score) in zip((back0, back1), picks):
            rows = lax.dot_general(pick, back[:, cols], (((0,), (0,)), ((), ())), preferred_element_type=F32)
            total = total + rows * score[:, None]
        return total

    theirs = swap(combine(slice(half, 2 * half)).astype(BF))
    return (combine(slice(0, half)) + theirs.astype(F32)).astype(BF)


def solution(mesh):
    placed = (
        P(("dp", "expert"), "et"),
        P(("dp", "expert"), None),
        P(("dp", "expert"), None),
        P("expert", None, ("dp", "et")),
        P("expert", None, ("dp", "et")),
        P("expert", "dp", "et"),
    )
    return jax.shard_map(
        on_device, mesh=mesh, in_specs=placed, out_specs=P(("dp", "expert"), "et"), check_vma=False
    )
```

```python
import jax
import jax.numpy as jnp
from jax import lax
from jax.experimental import pallas as pl
from jax.experimental.pallas import tpu as pltpu
from jax.sharding import PartitionSpec as P

SIDE = 4
BF = jnp.bfloat16
F32 = jnp.float32
VMEM_MB = 16


def plane_perm(first, step):
    pairs = []
    for y in range(SIDE):
        for x in range(SIDE):
            for c in range(2):
                along_x = (c == 0) == first
                ty, tx = (y, (x + step) % SIDE) if along_x else ((y + step) % SIDE, x)
                pairs.append(((y * SIDE + x) * 2 + c, (ty * SIDE + tx) * 2 + c))
    return pairs


def shift(a, first, step):
    return lax.ppermute(a, ("dp", "et"), plane_perm(first, step))


def swap(a):
    return lax.ppermute(a, "et", [(0, 1), (1, 0)])


def tie(value, *after):
    return lax.optimization_barrier((value, *after))[0]


def both(plus, minus, first):
    return shift(plus, first, 1), shift(minus, first, -1)


def add(*terms):
    total = terms[0].astype(F32)
    for t in terms[1:]:
        total = total + t.astype(F32)
    return total.astype(BF)


def ffn_body(core, *refs):
    c = core[0]
    wg0, wg1, wu0, wu1, wd0, wd1 = refs[:6]
    hidden = refs[-1]
    n_arrays = (len(refs) - 7) // 2
    ins, outs = refs[6:6 + n_arrays], refs[6 + n_arrays:-1]
    d = 2 * wd0.shape[1]
    half = d // 2
    hid = wg0.shape[1]
    mine = pl.multiple_of(c * half, half)
    other = pl.multiple_of((1 - c) * half, half)
    mine_h = pl.multiple_of(c * hid, hid)
    other_h = pl.multiple_of((1 - c) * hid, hid)
    lo, hi = pl.ds(0, half), pl.ds(half, half)
    at = 0
    while at < n_arrays:
        if ins[at].shape[1] == d:
            a, b = ins[at][:, lo], ins[at][:, hi]
            halves = [(outs[at], lo), (outs[at], hi)]
            at += 1
        else:
            a, b = ins[at][...], ins[at + 1][...]
            halves = [(outs[at], lo), (outs[at + 1], lo)]
            at += 2
        for k, (wg, wu) in enumerate(((wg0, wu0), (wg1, wu1))):
            def proj(w):
                return jnp.dot(a, w[pl.ds(mine, half), :], preferred_element_type=F32) + jnp.dot(
                    b, w[pl.ds(other, half), :], preferred_element_type=F32
                )

            g = proj(wg)
            u = proj(wu)
            hidden[:, pl.ds(k * hid, hid)] = (g / (1.0 + jnp.exp(-g)) * u).astype(BF)
        h0, h1 = hidden[:, pl.ds(0, hid)], hidden[:, pl.ds(hid, hid)]
        for (out, cols), w, first, second in zip(halves, (wd0, wd1), (mine_h, 0), (other_h, hid)):
            p = jnp.dot(h0, w[pl.ds(first, hid), :], preferred_element_type=F32) + jnp.dot(
                h1, w[pl.ds(second, hid), :], preferred_element_type=F32
            )
            out[:, cols] = p.astype(BF)


def ffn(core, weights, arrays):
    n = arrays[0].shape[0]
    half = weights[4].shape[1]
    hid = weights[0].shape[1]
    rows = sum(a.size for a in arrays) // (2 * half)
    whole = pl.BlockSpec(memory_space=pltpu.VMEM)
    return pl.pallas_call(
        ffn_body,
        in_specs=[pl.BlockSpec(memory_space=pltpu.SMEM)] + [whole] * (6 + len(arrays)),
        out_specs=[whole] * len(arrays),
        out_shape=[jax.ShapeDtypeStruct(a.shape, BF) for a in arrays],
        scratch_shapes=[pltpu.VMEM((n, 2 * hid), BF)],
        compiler_params=pltpu.CompilerParams(vmem_limit_bytes=VMEM_MB * 1024 * 1024),
        cost_estimate=pl.CostEstimate(
            flops=2 * rows * half * 2 * hid * 6, bytes_accessed=8 * rows * half + 24 * half * hid,
            transcendentals=2 * rows * hid,
        ),
        name="ffn",
    )(core, *weights, *arrays)


def on_device(tokens, expert_ids, gate_scores, w_gate, w_up, w_down):
    tok_rows, half = tokens.shape
    n_expert = lax.axis_size("expert")
    capacity = max(2, 5 * tok_rows // (2 * n_expert))
    z = lax.axis_index("expert")
    c = lax.axis_index("et")
    core = c.astype(jnp.int32).reshape(1)

    other_tokens = swap(tokens)
    t = jnp.arange(tok_rows, dtype=jnp.int32)
    slots = jnp.arange(capacity, dtype=jnp.int32)
    before = (t[:, None] < t[None, :]).astype(F32)

    def choose(e):
        named = expert_ids == e
        mask = jnp.any(named, axis=1)
        rank = jnp.dot(mask.astype(F32)[None, :], before, preferred_element_type=F32)[0].astype(jnp.int32)
        pick = (slots[:, None] == rank[None, :]) & mask[None, :]
        return pick.astype(BF), jnp.sum(jnp.where(named, gate_scores, 0.0), axis=1)

    send = [
        [(s * 2, (s + 2) % n_expert * 2) for s in range(n_expert)]
        + [(s * 2 + 1, (s + 1) % n_expert * 2 + 1) for s in range(n_expert)],
        [(s * 2, s * 2) for s in range(n_expert)] + [(s * 2 + 1, (s - 1) % n_expert * 2 + 1) for s in range(n_expert)],
    ]
    picks = [choose((z + 2 - c) % n_expert), choose((z - c) % n_expert)]

    pick_all = jnp.concatenate([pick for pick, _ in picks], axis=0)
    outgoing = jnp.concatenate(
        [jnp.dot(pick_all, v, preferred_element_type=F32).astype(BF) for v in (tokens, other_tokens)], axis=1
    )

    def dispatch(k, *after):
        rows = outgoing[k * capacity:(k + 1) * capacity]
        return lax.ppermute(tie(rows, *after) if after else rows, ("expert", "et"), send[k])

    def far_pair(left, right, first):
        return both(left[:, :half], right[:, half:], first)

    def fold(left, right, got_a, got_b):
        return (
            jnp.concatenate([left[:, :half], add(left[:, half:], got_b)], axis=1),
            jnp.concatenate([add(right[:, :half], got_a), right[:, half:]], axis=1),
        )

    z1 = dispatch(1)
    z0 = dispatch(0)
    weights = []
    for w in (w_gate[0], w_up[0], w_down[0]):
        weights += [w, swap(tie(w, other_tokens))]

    def collect(sums, *after):
        own, left, right, far = sums.reshape(SIDE, capacity, 2 * half)
        own = tie(own, *after) if after else own
        return add(own, shift(left, True, -1), shift(right, True, 1), shift(far, True, 2))

    own = tie(jnp.concatenate([z1, z0], axis=0), *weights)
    ring = (own, shift(own, True, 1), shift(own, True, -1), shift(own, True, 2))
    line0, line1 = [
        jnp.concatenate([p[k * capacity:(k + 1) * capacity] for p in ring], axis=0) for k in (1, 0)
    ]
    hid = w_gate.shape[2]
    down = tie(weights[5], own)
    weights[5] = jnp.where(c == 0, down, jnp.concatenate([down[hid:], down[:hid]], axis=0))
    left0, right0 = both(line0, line0, False)
    left1, right1 = both(line1, line1, False)
    (p_own0,) = ffn(core, weights, (line0,))
    (p_own1,) = ffn(core, weights, (line1,))
    left0, right0 = tie(left0, p_own0, p_own1), tie(right0, p_own0, p_own1)
    far_a0, far_b0 = far_pair(left0, right0, False)
    p_left0, p_right0 = ffn(core, weights, (left0, right0))
    far_a1, far_b1 = far_pair(tie(left1, p_left0), tie(right1, p_left0), False)
    p_left1, p_right1 = ffn(core, weights, (left1, right1))
    pf_a0, pf_b0 = ffn(core, weights, (tie(far_a0, p_left1), far_b0))
    got_a0, got_b0 = both(pf_a0, pf_b0, False)
    pf_a1, pf_b1 = ffn(core, weights, (tie(far_a1, pf_a0), far_b1))
    got_a1, got_b1 = both(pf_a1, pf_b1, False)
    sl0, sr0 = fold(p_left0, p_right0, got_a0, got_b0)
    from_l0, from_r0 = both(sr0, sl0, False)
    sl1, sr1 = fold(p_left1, p_right1, got_a1, got_b1)
    from_l1, from_r1 = both(sr1, sl1, False)
    done0 = collect(add(p_own0, from_l0, from_r0))
    back0 = lax.ppermute(done0, ("expert", "et"), [(b, a) for a, b in send[0]])
    done1 = collect(tie(add(p_own1, from_l1, from_r1), done0), back0)
    def combine(back, choice):
        pick, score = choice
        rows = lax.dot_general(pick, back, (((0,), (0,)), ((), ())), preferred_element_type=F32)
        return rows * score[:, None]

    theirs = swap(combine(back0[:, half:], picks[0]).astype(BF))
    done1 = tie(done1, theirs)
    kept = lax.ppermute(done1[:, :half], ("expert", "et"), [(b, a) for a, b in send[1]])
    crossed = lax.ppermute(done1[:, half:], ("expert", "et"), [(b, a ^ 1) for a, b in send[1]])

    total = combine(back0[:, :half], picks[0]) + theirs.astype(F32)
    total = total + combine(kept, picks[1]) + combine(crossed, choose((z - 1 + c) % n_expert))
    return total.astype(BF)


def solution(mesh):
    placed = (
        P(("dp", "expert"), "et"),
        P(("dp", "expert"), None),
        P(("dp", "expert"), None),
        P("expert", None, ("dp", "et")),
        P("expert", None, ("dp", "et")),
        P("expert", "dp", "et"),
    )
    return jax.shard_map(
        on_device, mesh=mesh, in_specs=placed, out_specs=P(("dp", "expert"), "et"), check_vma=False
    )
```
